32 devices in a mesh: dp: 2 (over core), tm: 4 (over z), space: 4 (over y, x).
Axes of the slice: x: 2, y: 2, z: 4, core: 2. Of those that a mesh axis runs over, the one named last changes fastest.
Arguments:
- latents: bfloat16 [2, 8, 8, 80, 512], P('dp', 'tm', 'space'), may hold values from -6 to 6
- norm_gain: float32 [512], replicated, may hold values from 0.25 to 1.75
- kernel: bfloat16 [13824, 512], P(None, 'dp'), may hold values from -0.0546875 to 0.0546875
- conv_bias: float32 [512], replicated, may hold values from -3 to 3
- out_grad: bfloat16 [2, 8, 8, 80, 512], P('dp', 'tm', 'space'), may hold values from -6 to 6
Outputs:
- block_out: bfloat16 [2, 8, 8, 80, 512], P('dp', 'tm', 'space')
- latent_grad: bfloat16 [2, 8, 8, 80, 512], P('dp', 'tm', 'space')
- kernel_grad: float32 [13824, 512], P('tm', 'dp')
- gain_grad: float32 [512], replicated
- bias_grad: float32 [512], replicated
The draws below stay inside these ranges and needn't reach their ends.
All inputs are finite; a program needn't handle non-finite values.
Results may differ from the reference program's by a relative error of at most 0.0029.
Values may be sent and summed in bfloat16 or wider, within the bound.
A program may use at most 128 MiB of HBM per device.

```python
import jax
import jax.numpy as jnp
from jax import lax

C = 512
TAPS = 27
W = 80
CLIPS = 2
FRAMES = 8
H = 8


def block_levels(stream_key, shape, split, least, high):
    level = 1.0
    for dim, shards_of in split:
        heights = jax.random.uniform(jax.random.fold_in(jax.random.fold_in(stream_key, 6), dim), (shards_of,), jnp.float32, least / len(split), high / len(split))
        level = level * jnp.repeat(jnp.exp(heights), shape[dim] // shards_of).reshape((-1,) + (1,) * (len(shape) - 1 - dim))
    return level


def centred(own_key, shape, width, limit, shards=(), held_as=jnp.bfloat16):
    entries = width * jax.random.normal(own_key, shape, jnp.float32)
    if shards:
        entries = entries * block_levels(own_key, shape, shards, -0.22, 0.18)
    return jnp.clip(entries, -limit, limit).astype(held_as)


def setup_inputs(seed: int = 0) -> dict:
    keys = jax.random.split(jax.random.key(seed), 6)
    return {
        "latents": centred(keys[0], (CLIPS, FRAMES, H, W, C), 1.0, 6.0, ((0, 2), (1, 4), (2, 4))),
        "norm_gain": jnp.clip(1.0 + 0.15 * jax.random.normal(keys[1], (C,), jnp.float32), 0.25, 1.75),
        "kernel": centred(keys[2], (TAPS * C, C), (TAPS * C) ** -0.5, 0.0546875, ((1, 2),)),
        "conv_bias": centred(keys[3], (C,), 0.5, 3.0, (), jnp.float32),
        "out_grad": centred(keys[4], (CLIPS, FRAMES, H, W, C), 1.0, 6.0, ((0, 2), (1, 4), (2, 4))),
    }


def reference(latents, norm_gain, kernel, conv_bias, out_grad):
    chans = latents.shape[-1]
    floats = latents.astype(jnp.float32)
    scale = 1.0 / jnp.sqrt(lax.optimization_barrier(jnp.mean(floats * floats, axis=-1, keepdims=True)) + 1e-06)
    normed = floats * scale
    pre_act = normed * norm_gain
    act = jax.nn.silu(pre_act).astype(jnp.bfloat16)
    blocks = kernel.reshape(3, 3, 3, chans, chans)
    clip_count, frame_count, row_count, col_count = latents.shape[:4]
    grad_scale = 1.0 / jnp.sqrt(jnp.float32(clip_count * frame_count * row_count * col_count))
    padded = jnp.pad(act, ((0, 0), (2, 0), (1, 1), (1, 1), (0, 0)))
    grad_pad = jnp.pad(out_grad, ((0, 0), (0, 2), (1, 1), (1, 1), (0, 0)))
    grad_flat = out_grad.reshape(-1, chans)
    conv = jnp.zeros(latents.shape, jnp.float32)
    act_grad = jnp.zeros(latents.shape, jnp.float32)
    kernel_rows = []
    for tap_t in range(3):
        for tap_h in range(3):
            for tap_w in range(3):
                window = padded[:, tap_t:tap_t + frame_count, tap_h:tap_h + row_count, tap_w:tap_w + col_count, :]
                window = window.reshape(-1, chans)
                conv = conv + jnp.dot(window, blocks[tap_t, tap_h, tap_w], preferred_element_type=jnp.float32).reshape(latents.shape)
                kernel_rows.append(jnp.dot(window.T, grad_flat, preferred_element_type=jnp.float32))
                back = grad_pad[:, 2 - tap_t:2 - tap_t + frame_count, 2 - tap_h:2 - tap_h + row_count, 2 - tap_w:2 - tap_w + col_count, :]
                act_grad = act_grad + jnp.dot(back.reshape(-1, chans), blocks[tap_t, tap_h, tap_w].T, preferred_element_type=jnp.float32).reshape(latents.shape)
    block_out = (floats + conv + conv_bias).astype(jnp.bfloat16)
    kernel_grad = jnp.concatenate(kernel_rows, axis=0) * grad_scale
    grads = out_grad.astype(jnp.float32)
    bias_grad = lax.optimization_barrier(jnp.sum(grads.reshape(-1, chans), axis=0)) * grad_scale
    sig = jax.nn.sigmoid(pre_act)
    pre_grad = act_grad * sig * (1.0 + pre_act * (1.0 - sig))
    gain_grad = lax.optimization_barrier(jnp.sum((pre_grad * normed).reshape(-1, chans), axis=0)) * grad_scale
    normed_grad = pre_grad * norm_gain
    latent_grad = grads + scale * (normed_grad - normed * lax.optimization_barrier(jnp.mean(normed_grad * normed, axis=-1, keepdims=True)))
    return (block_out, latent_grad.astype(jnp.bfloat16), kernel_grad, gain_grad, bias_grad)
```

```python
import functools

import jax
import jax.numpy as jnp
from jax import lax
from jax.experimental import pallas as pl
from jax.experimental.pallas import tpu as pltpu
from jax.sharding import PartitionSpec as P


def shifted(block, axis, distance):
    devices = range(lax.axis_size(axis))
    route = [(i - distance, i) for i in devices if i - distance in devices]
    return lax.ppermute(block, axis, route)


def padded(block, sides, width):
    for axis, dim in sides:
        count = lax.axis_size(axis)
        forward = [(i, i + 1) for i in range(count - 1)]
        backward = [(target, source) for source, target in forward]
        low = lax.ppermute(
            lax.slice_in_dim(block, block.shape[dim] - width, None, axis=dim), axis, forward
        )
        high = lax.ppermute(lax.slice_in_dim(block, 0, width, axis=dim), axis, backward)
        block = jnp.concatenate([low, block, high], axis=dim)
    return block


def tap_columns(extended, frame_count, row_count, col_count, flipped):
    pieces = []
    for tap_t in range(3):
        for tap_h in range(3):
            for tap_w in range(3):
                if flipped:
                    start_t, start_h, start_w = (2 - tap_t, 2 - tap_h, 2 - tap_w)
                else:
                    start_t, start_h, start_w = (tap_t, tap_h, tap_w)
                pieces.append(
                    extended[
                        :,
                        start_t : start_t + frame_count,
                        start_h : start_h + row_count,
                        start_w : start_w + col_count,
                        :,
                    ]
                )
    stacked = jnp.concatenate(pieces, axis=-1)
    return stacked.reshape(-1, stacked.shape[-1])


def pad_columns(extended):
    return jnp.pad(extended, ((0, 0), (0, 0), (0, 0), (1, 1), (0, 0)))


MESH = pl.DeviceIdType.MESH


def first_tap(owner, quarter, per, parts):
    return (per * owner - quarter + parts - 1) // parts


def reduce_spread_kernel(
    n, parts, per, slots, part_ref, out_ref, from_left, from_right, to_right, to_left, done,
    right_send, right_recv, left_send, left_recv, spread_send, spread_recv, own_sem,
):
    me_d, me_t, me_s = lax.axis_index("dp"), lax.axis_index("tm"), lax.axis_index("space")
    barrier = pltpu.get_barrier_semaphore()

    def signal(t, s):
        pl.semaphore_signal(barrier, inc=1, device_id=(me_d, t, s), device_id_type=MESH)

    for other in range(1, parts):
        signal(me_t, lax.rem(me_s + other, parts))

    @pl.when(me_t > 0)
    def _():
        signal(me_t - 1, me_s)

    @pl.when(me_t < n - 1)
    def _():
        signal(me_t + 1, me_s)

    ends = jnp.where(me_t > 0, 1, 0) + jnp.where(me_t < n - 1, 1, 0)
    pl.semaphore_wait(barrier, parts - 1 + ends)

    def mine(dest, slot):
        return part_ref[first_tap(dest, me_s, per, parts) + slot]

    def right_copy(dest, slot, target):
        return pltpu.make_async_remote_copy(
            src_ref=to_right.at[dest, slot], dst_ref=from_left.at[dest, slot],
            send_sem=right_send.at[dest, slot], recv_sem=right_recv.at[dest, slot],
            device_id=(me_d, target, me_s), device_id_type=MESH)

    def left_copy(dest, slot, target):
        return pltpu.make_async_remote_copy(
            src_ref=to_left.at[dest, slot], dst_ref=from_right.at[dest, slot],
            send_sem=left_send.at[dest, slot], recv_sem=left_recv.at[dest, slot],
            device_id=(me_d, target, me_s), device_id_type=MESH)

    offset = parts * first_tap(me_t, me_s, per, parts) + me_s - per * me_t

    def spread_copy(slot, other):
        unit = parts * slot + offset
        return pltpu.make_async_remote_copy(
            src_ref=done.at[slot], dst_ref=out_ref.at[unit],
            send_sem=spread_send.at[other - 1, slot], recv_sem=spread_recv.at[other - 1, slot],
            device_id=(me_d, me_t, lax.rem(me_s + other, parts)), device_id_type=MESH)

    def step(it, carry):
        r_slot = it - me_t
        l_slot = it - (n - 1 - me_t)
        f_slot = it - n
        for dist in range(n - 1, 0, -1):
            dest_r = me_t + dist
            dest_l = me_t - dist

            @pl.when((dest_r < n) & (r_slot >= 0) & (r_slot < slots))
            def _():
                @pl.when(me_t > 0)
                def _():
                    right_copy(dest_r, r_slot, me_t).wait_recv()
                    to_right[dest_r, r_slot] = (
                        from_left[dest_r, r_slot].astype(jnp.float32) + mine(dest_r, r_slot)
                    ).astype(jnp.bfloat16)

                @pl.when(me_t == 0)
                def _():
                    to_right[dest_r, r_slot] = mine(dest_r, r_slot).astype(jnp.bfloat16)

                right_copy(dest_r, r_slot, me_t + 1).start()

            @pl.when((dest_l >= 0) & (l_slot >= 0) & (l_slot < slots))
            def _():
                @pl.when(me_t < n - 1)
                def _():
                    left_copy(dest_l, l_slot, me_t).wait_recv()
                    to_left[dest_l, l_slot] = (
                        from_right[dest_l, l_slot].astype(jnp.float32) + mine(dest_l, l_slot)
                    ).astype(jnp.bfloat16)

                @pl.when(me_t == n - 1)
                def _():
                    to_left[dest_l, l_slot] = mine(dest_l, l_slot).astype(jnp.bfloat16)

                left_copy(dest_l, l_slot, me_t - 1).start()

        @pl.when(f_slot >= 0)
        def _():
            @pl.when(me_t == 0)
            def _():
                left_copy(me_t, f_slot, me_t).wait_recv()
                done[f_slot] = (
                    mine(me_t, f_slot) + from_right[me_t, f_slot].astype(jnp.float32)
                ).astype(jnp.bfloat16)

            @pl.when(me_t == n - 1)
            def _():
                right_copy(me_t, f_slot, me_t).wait_recv()
                done[f_slot] = (
                    mine(me_t, f_slot) + from_left[me_t, f_slot].astype(jnp.float32)
                ).astype(jnp.bfloat16)

            @pl.when((me_t > 0) & (me_t < n - 1))
            def _():
                left_copy(me_t, f_slot, me_t).wait_recv()
                right_copy(me_t, f_slot, me_t).wait_recv()
                done[f_slot] = (
                    mine(me_t, f_slot)
                    + from_left[me_t, f_slot].astype(jnp.float32)
                    + from_right[me_t, f_slot].astype(jnp.float32)
                ).astype(jnp.bfloat16)

            for other in range(1, parts):
                spread_copy(f_slot, other).start()
            pltpu.make_async_copy(
                done.at[f_slot], out_ref.at[parts * f_slot + offset], own_sem.at[f_slot]
            ).start()

        return carry

    lax.fori_loop(0, n + slots, step, 0)

    def drain(slot, carry):
        for dist in range(1, n):
            @pl.when(me_t + dist < n)
            def _():
                right_copy(me_t + dist, slot, me_t).wait_send()

            @pl.when(me_t - dist >= 0)
            def _():
                left_copy(me_t - dist, slot, me_t).wait_send()

        for other in range(1, parts):
            spread_copy(slot, other).wait()
        pltpu.make_async_copy(
            done.at[slot], out_ref.at[parts * slot + offset], own_sem.at[slot]
        ).wait()
        return carry

    lax.fori_loop(0, slots, drain, 0)


def reduce_spread(part, n, parts, per, slots):
    unit, cols = part.shape[1:]
    block = (n, slots, unit, cols)
    return pl.pallas_call(
        functools.partial(reduce_spread_kernel, n, parts, per, slots),
        out_shape=jax.ShapeDtypeStruct((parts * slots, unit, cols), jnp.bfloat16),
        in_specs=[pl.BlockSpec(memory_space=pltpu.VMEM)],
        out_specs=pl.BlockSpec(memory_space=pltpu.VMEM),
        scratch_shapes=[
            pltpu.VMEM(block, jnp.bfloat16),
            pltpu.VMEM(block, jnp.bfloat16),
            pltpu.VMEM(block, jnp.bfloat16),
            pltpu.VMEM(block, jnp.bfloat16),
            pltpu.VMEM((slots, unit, cols), jnp.bfloat16),
            pltpu.SemaphoreType.DMA((n, slots)),
            pltpu.SemaphoreType.DMA((n, slots)),
            pltpu.SemaphoreType.DMA((n, slots)),
            pltpu.SemaphoreType.DMA((n, slots)),
            pltpu.SemaphoreType.DMA((parts - 1, slots)),
            pltpu.SemaphoreType.DMA((parts - 1, slots)),
            pltpu.SemaphoreType.DMA((slots,)),
        ],
        compiler_params=pltpu.CompilerParams(
            collective_id=0, has_side_effects=True, vmem_limit_bytes=40 * 1024 * 1024
        ),
    )(part)


def on_device(latents, norm_gain, kernel, conv_bias, out_grad):
    chans = latents.shape[-1]
    half_cols = kernel.shape[1]
    clip_local, frame_count, row_count, col_count = (
        latents.shape[0],
        latents.shape[1],
        latents.shape[2],
        latents.shape[3],
    )
    cell_total = (
        clip_local
        * frame_count
        * row_count
        * col_count
        * lax.axis_size("dp")
        * lax.axis_size("tm")
        * lax.axis_size("space")
    )
    grad_scale = 1.0 / jnp.sqrt(jnp.float32(cell_total))
    floats = latents.astype(jnp.float32)
    scale = lax.rsqrt(jnp.mean(floats * floats, axis=-1, keepdims=True) + 1e-06)
    normed = floats * scale
    pre_act = normed * norm_gain
    act = jax.nn.silu(pre_act).astype(jnp.bfloat16)
    grad_pair = lax.all_to_all(out_grad, "dp", split_axis=4, concat_axis=0, tiled=True)
    earlier = shifted(act, "tm", 1)
    joined = jnp.concatenate([earlier, act], axis=1)
    act_ext = padded(joined, (("space", 2),), 1)
    later = shifted(grad_pair, "tm", -1)
    joined_grad = jnp.concatenate([grad_pair, later], axis=1)
    grad_ext = padded(joined_grad, (("space", 2),), 1)
    act_pair = lax.all_gather(act_ext, "dp", axis=0, tiled=True)
    pair_clips = act_pair.shape[0]
    act_taps = tap_columns(pad_columns(act_pair), frame_count, row_count, col_count, False)
    conv_part = jnp.dot(act_taps, kernel, preferred_element_type=jnp.float32)
    conv_part = conv_part.reshape(pair_clips, frame_count, row_count, col_count, half_cols)
    conv = lax.all_to_all(conv_part, "dp", split_axis=0, concat_axis=4, tiled=True)
    block_out = (floats + conv + conv_bias).astype(jnp.bfloat16)
    n_tm, n_space = lax.axis_size("tm"), lax.axis_size("space")
    units = 27 * n_space
    split = n_tm > 1 and n_space > 1 and chans % (128 * n_space) == 0 and units % n_tm == 0
    if split:
        unit, per = chans // n_space, units // n_tm
        slots = -(-per // n_space)
        act_part = lax.all_to_all(joined, "space", split_axis=4, concat_axis=2, tiled=True)
        act_rows = lax.all_gather(act_part, "dp", axis=0, tiled=True)
        act_rows = jnp.pad(act_rows, ((0, 0), (0, 0), (1, 1), (1, 1), (0, 0)))
        grad_rows = lax.all_gather(grad_pair, "space", axis=2, tiled=True)
        row_taps = tap_columns(act_rows, frame_count, row_count * n_space, col_count, False)
        part = (
            lax.dot_general(
                row_taps,
                grad_rows.reshape(-1, half_cols),
                (((0,), (0,)), ((), ())),
                preferred_element_type=jnp.float32,
            )
            * grad_scale
        )
        part = jnp.pad(part.reshape(27, unit, half_cols), ((0, 1), (0, 0), (0, 0)))
        spread = reduce_spread(part, n_tm, n_space, per, slots)
        kernel_grad = spread.reshape(-1, half_cols)[: per * unit].astype(jnp.float32)
    else:
        kernel_local = (
            lax.dot_general(
                act_taps,
                grad_pair.reshape(-1, half_cols),
                (((0,), (0,)), ((), ())),
                preferred_element_type=jnp.float32,
            )
            * grad_scale
        )
        col_part = lax.psum_scatter(kernel_local, "space", scatter_dimension=1, tiled=True)
        cell_part = lax.psum_scatter(col_part, "tm", scatter_dimension=0, tiled=True)
        kernel_grad = lax.all_gather(cell_part, "space", axis=1, tiled=True)
    flipped_kernel = jnp.transpose(kernel.reshape(-1, chans, half_cols), (0, 2, 1)).reshape(
        -1, chans
    )
    grad_taps = tap_columns(pad_columns(grad_ext), frame_count, row_count, col_count, True)
    partial_grad = jnp.dot(grad_taps, flipped_kernel, preferred_element_type=jnp.float32)
    partial_grad = partial_grad.reshape(pair_clips, frame_count, row_count, col_count, chans)
    act_grad = lax.psum_scatter(partial_grad, "dp", scatter_dimension=0, tiled=True)
    grads = out_grad.astype(jnp.float32)
    bias_local = jnp.sum(grads.reshape(-1, chans), axis=0) * grad_scale
    sig = jax.nn.sigmoid(pre_act)
    pre_grad = act_grad * sig * (1.0 + pre_act * (1.0 - sig))
    gain_local = jnp.sum((pre_grad * normed).reshape(-1, chans), axis=0) * grad_scale
    normed_grad = pre_grad * norm_gain
    latent_grad = grads + scale * (
        normed_grad - normed * jnp.mean(normed_grad * normed, axis=-1, keepdims=True)
    )
    gain_grad, bias_grad = lax.psum((gain_local, bias_local), ("dp", "tm", "space"))
    return (block_out, latent_grad.astype(jnp.bfloat16), kernel_grad, gain_grad, bias_grad)


def solution(mesh):
    in_specs = (
        P("dp", "tm", "space", None, None),
        P(),
        P(None, "dp"),
        P(),
        P("dp", "tm", "space", None, None),
    )
    out_specs = (
        P("dp", "tm", "space", None, None),
        P("dp", "tm", "space", None, None),
        P("tm", "dp"),
        P(),
        P(),
    )
    return jax.shard_map(
        on_device, mesh=mesh, in_specs=in_specs, out_specs=out_specs, check_vma=False
    )
```

```python
import functools
import math

import jax
import jax.numpy as jnp
from jax import lax
from jax.experimental import pallas as pl
from jax.experimental.pallas import tpu as pltpu
from jax.sharding import PartitionSpec as P


def shifted(block, axis, distance):
    devices = range(lax.axis_size(axis))
    route = [(i - distance, i) for i in devices if i - distance in devices]
    return lax.ppermute(block, axis, route)


def padded(block, sides, width):
    for axis, dim in sides:
        count = lax.axis_size(axis)
        forward = [(i, i + 1) for i in range(count - 1)]
        backward = [(target, source) for source, target in forward]
        low = lax.ppermute(
            lax.slice_in_dim(block, block.shape[dim] - width, None, axis=dim), axis, forward
        )
        high = lax.ppermute(lax.slice_in_dim(block, 0, width, axis=dim), axis, backward)
        block = jnp.concatenate([low, block, high], axis=dim)
    return block


def tap_columns(extended, frame_count, row_count, col_count, flipped):
    pieces = []
    for tap_t in range(3):
        for tap_h in range(3):
            for tap_w in range(3):
                if flipped:
                    start_t, start_h, start_w = (2 - tap_t, 2 - tap_h, 2 - tap_w)
                else:
                    start_t, start_h, start_w = (tap_t, tap_h, tap_w)
                pieces.append(
                    extended[
                        :,
                        start_t : start_t + frame_count,
                        start_h : start_h + row_count,
                        start_w : start_w + col_count,
                        :,
                    ]
                )
    stacked = jnp.concatenate(pieces, axis=-1)
    return stacked.reshape(-1, stacked.shape[-1])


def pad_columns(extended):
    return jnp.pad(extended, ((0, 0), (0, 0), (0, 0), (1, 1), (0, 0)))


MESH = pl.DeviceIdType.MESH


def first_tap(owner, quarter, per, parts):
    return (per * owner - quarter + parts - 1) // parts


def greet(n, parts):
    me_d, me_t, me_s = lax.axis_index("dp"), lax.axis_index("tm"), lax.axis_index("space")
    barrier = pltpu.get_barrier_semaphore()

    def signal(d, t, s):
        pl.semaphore_signal(barrier, inc=1, device_id=(d, t, s), device_id_type=MESH)

    for other in range(1, parts):
        signal(me_d, me_t, lax.rem(me_s + other, parts))
    for other in range(1, n):
        signal(me_d, lax.rem(me_t + other, n), me_s)
    signal(1 - me_d, me_t, me_s)
    pl.semaphore_wait(barrier, parts + n - 1)
    return me_d, me_t, me_s


def reduce_spread_kernel(
    n, parts, per, slots, grad_scale, act_ref, cot_ref, vec_ref, out_ref, vec_out,
    part_ref, from_left, from_right, to_right, to_left, done, vec_plane, vec_line, vec_pair,
    right_send, right_recv, left_send, left_recv, spread_send, spread_recv, own_sem,
    plane_send, plane_recv, line_send, line_recv, pair_send, pair_recv,
):
    me_d, me_t, me_s = greet(n, parts)
    half = out_ref.shape[-1]
    frames, rows = act_ref.shape[1] // 2, act_ref.shape[2] - 2

    def plane_copy(other):
        return pltpu.make_async_remote_copy(
            src_ref=vec_ref, dst_ref=vec_plane.at[me_s],
            send_sem=plane_send.at[other - 1], recv_sem=plane_recv.at[other - 1],
            device_id=(me_d, me_t, lax.rem(me_s + other, parts)), device_id_type=MESH)

    def line_copy(other):
        return pltpu.make_async_remote_copy(
            src_ref=vec_line.at[me_t], dst_ref=vec_line.at[me_t],
            send_sem=line_send.at[other - 1], recv_sem=line_recv.at[other - 1],
            device_id=(me_d, lax.rem(me_t + other, n), me_s), device_id_type=MESH)

    pair_copy = pltpu.make_async_remote_copy(
        src_ref=vec_pair.at[0], dst_ref=vec_pair.at[1],
        send_sem=pair_send, recv_sem=pair_recv,
        device_id=(1 - me_d, me_t, me_s), device_id_type=MESH)

    for other in range(1, parts):
        plane_copy(other).start()
    vec_plane[me_s] = vec_ref[...]

    for tap_t in range(3):
        for tap_h in range(3):
            total = None
            for clip in range(2):
                window = act_ref[clip, tap_t : tap_t + frames, tap_h : tap_h + rows]
                term = lax.dot_general(
                    window.reshape(-1, window.shape[-1]), cot_ref[clip],
                    (((0,), (0,)), ((), ())), preferred_element_type=jnp.float32)
                total = term if total is None else total + term
            total = total * grad_scale
            for tap_w in range(3):
                part_ref[9 * tap_t + 3 * tap_h + tap_w] = total[
                    :, tap_w * half : (tap_w + 1) * half
                ]
    part_ref[27] = jnp.zeros_like(part_ref[27])

    for other in range(1, parts):
        plane_copy(other).wait()
    vec_line[me_t] = functools.reduce(lambda a, b: a + b, [vec_plane[i] for i in range(parts)])
    for other in range(1, n):
        line_copy(other).start()

    def mine(dest, slot):
        return part_ref[first_tap(dest, me_s, per, parts) + slot]

    def right_copy(dest, slot, target):
        return pltpu.make_async_remote_copy(
            src_ref=to_right.at[dest, slot], dst_ref=from_left.at[dest, slot],
            send_sem=right_send.at[dest, slot], recv_sem=right_recv.at[dest, slot],
            device_id=(me_d, target, me_s), device_id_type=MESH)

    def left_copy(dest, slot, target):
        return pltpu.make_async_remote_copy(
            src_ref=to_left.at[dest, slot], dst_ref=from_right.at[dest, slot],
            send_sem=left_send.at[dest, slot], recv_sem=left_recv.at[dest, slot],
            device_id=(me_d, target, me_s), device_id_type=MESH)

    offset = parts * first_tap(me_t, me_s, per, parts) + me_s - per * me_t

    def spread_copy(slot, other):
        unit = parts * slot + offset
        return pltpu.make_async_remote_copy(
            src_ref=done.at[slot], dst_ref=out_ref.at[unit],
            send_sem=spread_send.at[other - 1, slot], recv_sem=spread_recv.at[other - 1, slot],
            device_id=(me_d, me_t, lax.rem(me_s + other, parts)), device_id_type=MESH)

    def step(it, carry):
        r_slot = it - me_t
        l_slot = it - (n - 1 - me_t)
        f_slot = it - n
        for dist in range(n - 1, 0, -1):
            dest_r = me_t + dist
            dest_l = me_t - dist

            @pl.when((dest_r < n) & (r_slot >= 0) & (r_slot < slots))
            def _():
                @pl.when(me_t > 0)
                def _():
                    right_copy(dest_r, r_slot, me_t).wait_recv()
                    to_right[dest_r, r_slot] = (
                        from_left[dest_r, r_slot].astype(jnp.float32) + mine(dest_r, r_slot)
                    ).astype(jnp.bfloat16)

                @pl.when(me_t == 0)
                def _():
                    to_right[dest_r, r_slot] = mine(dest_r, r_slot).astype(jnp.bfloat16)

                right_copy(dest_r, r_slot, me_t + 1).start()

            @pl.when((dest_l >= 0) & (l_slot >= 0) & (l_slot < slots))
            def _():
                @pl.when(me_t < n - 1)
                def _():
                    left_copy(dest_l, l_slot, me_t).wait_recv()
                    to_left[dest_l, l_slot] = (
                        from_right[dest_l, l_slot].astype(jnp.float32) + mine(dest_l, l_slot)
                    ).astype(jnp.bfloat16)

                @pl.when(me_t == n - 1)
                def _():
                    to_left[dest_l, l_slot] = mine(dest_l, l_slot).astype(jnp.bfloat16)

                left_copy(dest_l, l_slot, me_t - 1).start()

        @pl.when(f_slot >= 0)
        def _():
            @pl.when(me_t == 0)
            def _():
                left_copy(me_t, f_slot, me_t).wait_recv()
                done[f_slot] = (
                    mine(me_t, f_slot) + from_right[me_t, f_slot].astype(jnp.float32)
                ).astype(jnp.bfloat16)

            @pl.when(me_t == n - 1)
            def _():
                right_copy(me_t, f_slot, me_t).wait_recv()
                done[f_slot] = (
                    mine(me_t, f_slot) + from_left[me_t, f_slot].astype(jnp.float32)
                ).astype(jnp.bfloat16)

            @pl.when((me_t > 0) & (me_t < n - 1))
            def _():
                left_copy(me_t, f_slot, me_t).wait_recv()
                right_copy(me_t, f_slot, me_t).wait_recv()
                done[f_slot] = (
                    mine(me_t, f_slot)
                    + from_left[me_t, f_slot].astype(jnp.float32)
                    + from_right[me_t, f_slot].astype(jnp.float32)
                ).astype(jnp.bfloat16)

            for other in range(1, parts):
                spread_copy(f_slot, other).start()
            pltpu.make_async_copy(
                done.at[f_slot], out_ref.at[parts * f_slot + offset], own_sem.at[f_slot]
            ).start()

        return carry

    lax.fori_loop(0, n + slots, step, 0)

    for other in range(1, n):
        line_copy(other).wait()
    vec_pair[0] = functools.reduce(lambda a, b: a + b, [vec_line[i] for i in range(n)])
    pair_copy.start()

    def drain(slot, carry):
        for dist in range(1, n):
            @pl.when(me_t + dist < n)
            def _():
                right_copy(me_t + dist, slot, me_t).wait_send()

            @pl.when(me_t - dist >= 0)
            def _():
                left_copy(me_t - dist, slot, me_t).wait_send()

        for other in range(1, parts):
            spread_copy(slot, other).wait()
        pltpu.make_async_copy(
            done.at[slot], out_ref.at[parts * slot + offset], own_sem.at[slot]
        ).wait()
        return carry

    lax.fori_loop(0, slots, drain, 0)
    pair_copy.wait()
    vec_out[...] = vec_pair[0] + vec_pair[1]


def reduce_spread(act_rows, cot_rows, vec, n, parts, per, slots, grad_scale):
    unit, cols = act_rows.shape[-1], cot_rows.shape[-1] // 3
    block = (n, slots, unit, cols)
    dma = pltpu.SemaphoreType.DMA
    vmem = pl.BlockSpec(memory_space=pltpu.VMEM)
    return pl.pallas_call(
        functools.partial(reduce_spread_kernel, n, parts, per, slots, grad_scale),
        out_shape=(
            jax.ShapeDtypeStruct((parts * slots, unit, cols), jnp.bfloat16),
            jax.ShapeDtypeStruct(vec.shape, jnp.float32),
        ),
        in_specs=[vmem] * 3,
        out_specs=(vmem, vmem),
        scratch_shapes=[pltpu.VMEM((28, unit, cols), jnp.float32)]
        + [pltpu.VMEM(block, jnp.bfloat16)] * 4
        + [
            pltpu.VMEM((slots, unit, cols), jnp.bfloat16),
            pltpu.VMEM((parts,) + vec.shape, jnp.float32),
            pltpu.VMEM((n,) + vec.shape, jnp.float32),
            pltpu.VMEM((2,) + vec.shape, jnp.float32),
        ]
        + [dma((n, slots))] * 4
        + [dma((parts - 1, slots))] * 2
        + [dma((slots,))]
        + [dma((parts - 1,))] * 2
        + [dma((n - 1,))] * 2
        + [dma, dma],
        compiler_params=pltpu.CompilerParams(
            collective_id=0, has_side_effects=True, vmem_limit_bytes=48 * 1024 * 1024
        ),
    )(act_rows, cot_rows, vec)


def exchange_kernel(n, parts, act_ref, grad_ref, af, aq, gr, gn, send, recv, local):
    me_d, me_t, me_s = greet(n, parts)
    frames, rows, _, chans = act_ref.shape
    half, quarter = gr.shape[-1], aq.shape[-1]
    before, now = pl.ds(0, frames), pl.ds(frames, frames)
    inner = pl.ds(1, rows)
    own = pl.ds(1 + me_s * rows, rows)
    last = 1 + parts * rows

    def channels(index, size):
        return pl.ds(pl.multiple_of(index * size, size), size)

    def remote(i, src, dst, d, t, s):
        return pltpu.make_async_remote_copy(
            src_ref=src, dst_ref=dst, send_sem=send.at[i], recv_sem=recv.at[i],
            device_id=(d, t, s), device_id_type=MESH)

    partner = (1 - me_d, me_t, me_s)
    peers = [lax.rem(me_s + other, parts) for other in range(1, parts)]

    first = 0
    to_partner = remote(
        first, grad_ref.at[:, :, :, channels(1 - me_d, half)], gr.at[me_d, :, own], *partner)
    to_partner.start()
    later = remote(1, act_ref, af.at[me_d, before, inner], me_d, me_t + 1, me_s)

    @pl.when(me_t < n - 1)
    def _():
        later.start()

    def quarter_copy(i, peer, source, when):
        return remote(
            i, source.at[:, :, :, channels(peer, quarter)], aq.at[me_d, when, own],
            me_d, me_t, peer)

    def edge_down(i, source, row, dst):
        return remote(i, source.at[:, row], dst, me_d, me_t, me_s + 1)

    def edge_up(i, source, row, dst):
        return remote(i, source.at[:, row], dst, me_d, me_t, me_s - 1)

    base = 2
    quarters_now = [quarter_copy(base + i, peer, act_ref, now) for i, peer in enumerate(peers)]
    base += parts - 1
    down_now = edge_down(base, act_ref, rows - 1, af.at[me_d, now, 0])
    up_now = edge_up(base + 1, act_ref, 0, af.at[me_d, now, rows + 1])
    base += 2
    own_rows = gr.at[:, :, own]
    gather = [remote(base + i, own_rows, own_rows, me_d, me_t, peer) for i, peer in enumerate(peers)]
    base += parts - 1
    sooner = remote(base, own_rows, gn.at[:, :, inner], me_d, me_t - 1, me_s)
    base += 1
    past = af.at[me_d, before, inner]
    quarters_before = [quarter_copy(base + i, peer, past, before) for i, peer in enumerate(peers)]
    base += parts - 1
    down_before = edge_down(base, past, rows - 1, af.at[me_d, before, 0])
    up_before = edge_up(base + 1, past, 0, af.at[me_d, before, rows + 1])
    base += 2
    down_next = edge_down(base, gn.at[0], rows, gn.at[0, :, 0])
    down_next2 = edge_down(base + 1, gn.at[1], rows, gn.at[1, :, 0])
    up_next = edge_up(base + 2, gn.at[0], 1, gn.at[0, :, rows + 1])
    up_next2 = edge_up(base + 3, gn.at[1], 1, gn.at[1, :, rows + 1])
    base += 4
    forward = [
        remote(base + i, ref.at[me_d, when], ref.at[me_d, when], *partner)
        for i, (ref, when) in enumerate(((aq, now), (af, now), (aq, before), (af, before)))
    ]

    keep = [
        pltpu.make_async_copy(
            grad_ref.at[:, :, :, channels(me_d, half)], gr.at[me_d, :, own], local.at[0]),
        pltpu.make_async_copy(
            act_ref.at[:, :, :, channels(me_s, quarter)], aq.at[me_d, now, own], local.at[1]),
        pltpu.make_async_copy(act_ref, af.at[me_d, now, inner], local.at[2]),
    ]
    keep_before = pltpu.make_async_copy(
        past.at[:, :, :, channels(me_s, quarter)], aq.at[me_d, before, own], local.at[3])

    below, above = me_s < parts - 1, me_s > 0
    for copy in keep:
        copy.start()
    for copy in quarters_now:
        copy.start()

    def start_if(condition, *copies):
        @pl.when(condition)
        def _():
            for copy in copies:
                copy.start()

    start_if(below, down_now)
    start_if(above, up_now)

    def clear(ref, *index):
        ref[index] = jnp.zeros(ref.at[index].shape, ref.dtype)

    everything = slice(None)
    for row in (0, last):
        clear(gr, everything, everything, row)
        clear(aq, me_d, everything, row)

    @pl.when(me_s == 0)
    def _():
        clear(af, me_d, everything, 0)
        clear(gn, everything, everything, 0)

    @pl.when(me_s == parts - 1)
    def _():
        clear(af, me_d, everything, rows + 1)
        clear(gn, everything, everything, rows + 1)

    to_partner.wait_recv()
    keep[0].wait()
    start_if(me_t > 0, sooner)
    for copy in gather:
        copy.start()

    @pl.when(me_t > 0)
    def _():
        later.wait_recv()
        keep_before.start()
        for copy in quarters_before:
            copy.start()
        start_if(below, down_before)
        start_if(above, up_before)

    @pl.when(me_t == 0)
    def _():
        clear(aq, me_d, before, pl.ds(1, parts * rows))
        clear(af, me_d, before, inner)

        @pl.when(above)
        def _():
            clear(af, me_d, before, 0)

        @pl.when(below)
        def _():
            clear(af, me_d, before, rows + 1)

    keep[1].wait()
    keep[2].wait()
    for copy in quarters_now:
        copy.wait_recv()

    def received(condition, *copies):
        @pl.when(condition)
        def _():
            for copy in copies:
                copy.wait_recv()

    received(above, down_now)
    received(below, up_now)
    forward[0].start()
    forward[1].start()

    @pl.when(me_t < n - 1)
    def _():
        sooner.wait_recv()
        start_if(below, down_next, down_next2)
        start_if(above, up_next, up_next2)

    @pl.when(me_t == n - 1)
    def _():
        clear(gn, everything, everything, inner)

        @pl.when(above)
        def _():
            clear(gn, everything, everything, 0)

        @pl.when(below)
        def _():
            clear(gn, everything, everything, rows + 1)

    @pl.when(me_t > 0)
    def _():
        keep_before.wait()
        for copy in quarters_before:
            copy.wait_recv()
        received(above, down_before)
        received(below, up_before)

    forward[2].start()
    forward[3].start()

    @pl.when(me_t < n - 1)
    def _():
        received(above, down_next, down_next2)
        received(below, up_next, up_next2)

    for copy in gather:
        copy.wait_recv()
    for copy in forward:
        copy.wait_recv()

    def sent(condition, *copies):
        @pl.when(condition)
        def _():
            for copy in copies:
                copy.wait_send()

    for copy in [to_partner] + quarters_now + gather + forward:
        copy.wait_send()
    sent(below, down_now)
    sent(above, up_now)
    sent(me_t < n - 1, later)
    sent(me_t > 0, sooner, *quarters_before)
    sent((me_t > 0) & below, down_before)
    sent((me_t > 0) & above, up_before)
    sent((me_t < n - 1) & below, down_next, down_next2)
    sent((me_t < n - 1) & above, up_next, up_next2)


def exchange(act, grad, n, parts):
    frames, rows, cols, chans = act.shape
    half, quarter = chans // 2, chans // parts
    messages = 4 * (parts - 1) + 15
    dma = pltpu.SemaphoreType.DMA
    vmem = pl.BlockSpec(memory_space=pltpu.VMEM)
    return pl.pallas_call(
        functools.partial(exchange_kernel, n, parts),
        out_shape=(
            jax.ShapeDtypeStruct((2, 2 * frames, rows + 2, cols, chans), jnp.bfloat16),
            jax.ShapeDtypeStruct((2, 2 * frames, parts * rows + 2, cols, quarter), jnp.bfloat16),
            jax.ShapeDtypeStruct((2, frames, parts * rows + 2, cols, half), jnp.bfloat16),
            jax.ShapeDtypeStruct((2, frames, rows + 2, cols, half), jnp.bfloat16),
        ),
        in_specs=[vmem] * 2,
        out_specs=(vmem,) * 4,
        scratch_shapes=[dma((messages,)), dma((messages,)), dma((4,))],
        compiler_params=pltpu.CompilerParams(
            collective_id=1, has_side_effects=True, vmem_limit_bytes=32 * 1024 * 1024
        ),
    )(act, grad)


def split_over_space(latents, norm_gain, kernel, conv_bias, out_grad):
    chans, half_cols = latents.shape[-1], kernel.shape[1]
    _, frame_count, row_count, col_count = latents.shape[:4]
    n_tm, n_space = lax.axis_size("tm"), lax.axis_size("space")
    cell_total = frame_count * row_count * col_count * 2 * n_tm * n_space
    grad_scale = 1.0 / math.sqrt(cell_total)
    unit, per = chans // n_space, 27 * n_space // n_tm
    slots = -(-per // n_space)

    floats = latents.astype(jnp.float32)
    scale = lax.rsqrt(jnp.mean(floats * floats, axis=-1, keepdims=True) + 1e-06)
    normed = floats * scale
    pre_act = normed * norm_gain
    act = jax.nn.silu(pre_act).astype(jnp.bfloat16)
    act_pair, act_rows, grad_rows, grad_next = exchange(act[0], out_grad[0], n_tm, n_space)

    act_taps = tap_columns(pad_columns(act_pair), frame_count, row_count, col_count, False)
    conv_part = jnp.dot(act_taps, kernel, preferred_element_type=jnp.float32)
    conv_part = conv_part.reshape(2, frame_count, row_count, col_count, half_cols)
    conv = lax.all_to_all(conv_part, "dp", split_axis=0, concat_axis=4, tiled=True)
    block_out = (floats + conv + conv_bias).astype(jnp.bfloat16)

    mine = lax.dynamic_slice_in_dim(
        grad_rows, lax.axis_index("space") * row_count, row_count + 2, axis=2)
    grad_ext = jnp.concatenate([mine, grad_next], axis=1)
    flipped_kernel = jnp.transpose(kernel.reshape(-1, chans, half_cols), (0, 2, 1)).reshape(
        -1, chans
    )
    grad_taps = tap_columns(pad_columns(grad_ext), frame_count, row_count, col_count, True)
    partial_grad = jnp.dot(grad_taps, flipped_kernel, preferred_element_type=jnp.float32)
    partial_grad = partial_grad.reshape(2, frame_count, row_count, col_count, chans)
    act_grad = lax.psum_scatter(partial_grad, "dp", scatter_dimension=0, tiled=True)

    grads = out_grad.astype(jnp.float32)
    bias_local = jnp.sum(grads.reshape(-1, chans), axis=0) * grad_scale
    sig = jax.nn.sigmoid(pre_act)
    pre_grad = act_grad * sig * (1.0 + pre_act * (1.0 - sig))
    gain_local = jnp.sum((pre_grad * normed).reshape(-1, chans), axis=0) * grad_scale
    normed_grad = pre_grad * norm_gain
    latent_grad = grads + scale * (
        normed_grad - normed * jnp.mean(normed_grad * normed, axis=-1, keepdims=True)
    )

    wide = jnp.pad(grad_rows[:, :, 1:-1], ((0, 0), (0, 0), (0, 0), (1, 1), (0, 0)))
    cot_rows = jnp.concatenate(
        [wide[..., 2 - tap : 2 - tap + col_count, :] for tap in range(3)], axis=-1
    ).reshape(2, -1, 3 * half_cols)
    vec = jnp.concatenate([gain_local, bias_local]).reshape(-1, 128)
    spread, vec = reduce_spread(
        act_rows, cot_rows, vec, n_tm, n_space, per, slots, grad_scale)
    kernel_grad = spread.reshape(-1, half_cols)[: per * unit].astype(jnp.float32)
    gain_grad, bias_grad = vec.reshape(2, chans)
    return (block_out, latent_grad.astype(jnp.bfloat16), kernel_grad, gain_grad, bias_grad)


def on_device(latents, norm_gain, kernel, conv_bias, out_grad):
    chans = latents.shape[-1]
    n_tm, n_space = lax.axis_size("tm"), lax.axis_size("space")
    splits = (
        lax.axis_size("dp") == 2
        and n_tm > 1
        and n_space > 1
        and latents.shape[:2] == (1, 2)
        and chans % (128 * n_space) == 0
        and chans % 256 == 0
        and latents.shape[3] % 16 == 0
        and 27 * n_space % n_tm == 0
    )
    path = split_over_space if splits else general
    return path(latents, norm_gain, kernel, conv_bias, out_grad)


def general(latents, norm_gain, kernel, conv_bias, out_grad):
    chans = latents.shape[-1]
    half_cols = kernel.shape[1]
    clip_local, frame_count, row_count, col_count = (
        latents.shape[0],
        latents.shape[1],
        latents.shape[2],
        latents.shape[3],
    )
    cell_total = (
        clip_local
        * frame_count
        * row_count
        * col_count
        * lax.axis_size("dp")
        * lax.axis_size("tm")
        * lax.axis_size("space")
    )
    grad_scale = 1.0 / jnp.sqrt(jnp.float32(cell_total))
    floats = latents.astype(jnp.float32)
    scale = lax.rsqrt(jnp.mean(floats * floats, axis=-1, keepdims=True) + 1e-06)
    normed = floats * scale
    pre_act = normed * norm_gain
    act = jax.nn.silu(pre_act).astype(jnp.bfloat16)
    grad_pair = lax.all_to_all(out_grad, "dp", split_axis=4, concat_axis=0, tiled=True)
    earlier = shifted(act, "tm", 1)
    joined = jnp.concatenate([earlier, act], axis=1)
    act_ext = padded(joined, (("space", 2),), 1)
    later = shifted(grad_pair, "tm", -1)
    joined_grad = jnp.concatenate([grad_pair, later], axis=1)
    grad_ext = padded(joined_grad, (("space", 2),), 1)
    act_pair = lax.all_gather(act_ext, "dp", axis=0, tiled=True)
    pair_clips = act_pair.shape[0]
    act_taps = tap_columns(pad_columns(act_pair), frame_count, row_count, col_count, False)
    conv_part = jnp.dot(act_taps, kernel, preferred_element_type=jnp.float32)
    conv_part = conv_part.reshape(pair_clips, frame_count, row_count, col_count, half_cols)
    conv = lax.all_to_all(conv_part, "dp", split_axis=0, concat_axis=4, tiled=True)
    block_out = (floats + conv + conv_bias).astype(jnp.bfloat16)
    kernel_local = (
        lax.dot_general(
            act_taps,
            grad_pair.reshape(-1, half_cols),
            (((0,), (0,)), ((), ())),
            preferred_element_type=jnp.float32,
        )
        * grad_scale
    )
    flipped_kernel = jnp.transpose(kernel.reshape(-1, chans, half_cols), (0, 2, 1)).reshape(
        -1, chans
    )
    grad_taps = tap_columns(pad_columns(grad_ext), frame_count, row_count, col_count, True)
    partial_grad = jnp.dot(grad_taps, flipped_kernel, preferred_element_type=jnp.float32)
    partial_grad = partial_grad.reshape(pair_clips, frame_count, row_count, col_count, chans)
    act_grad = lax.psum_scatter(partial_grad, "dp", scatter_dimension=0, tiled=True)
    grads = out_grad.astype(jnp.float32)
    bias_local = jnp.sum(grads.reshape(-1, chans), axis=0) * grad_scale
    sig = jax.nn.sigmoid(pre_act)
    pre_grad = act_grad * sig * (1.0 + pre_act * (1.0 - sig))
    gain_local = jnp.sum((pre_grad * normed).reshape(-1, chans), axis=0) * grad_scale
    normed_grad = pre_grad * norm_gain
    latent_grad = grads + scale * (
        normed_grad - normed * jnp.mean(normed_grad * normed, axis=-1, keepdims=True)
    )
    gain_grad, bias_grad = lax.psum((gain_local, bias_local), ("dp", "tm", "space"))
    col_part = lax.psum_scatter(kernel_local, "space", scatter_dimension=1, tiled=True)
    cell_part = lax.psum_scatter(col_part, "tm", scatter_dimension=0, tiled=True)
    kernel_grad = lax.all_gather(cell_part, "space", axis=1, tiled=True)
    return (block_out, latent_grad.astype(jnp.bfloat16), kernel_grad, gain_grad, bias_grad)


def solution(mesh):
    in_specs = (
        P("dp", "tm", "space", None, None),
        P(),
        P(None, "dp"),
        P(),
        P("dp", "tm", "space", None, None),
    )
    out_specs = (
        P("dp", "tm", "space", None, None),
        P("dp", "tm", "space", None, None),
        P("tm", "dp"),
        P(),
        P(),
    )
    return jax.shard_map(
        on_device, mesh=mesh, in_specs=in_specs, out_specs=out_specs, check_vma=False
    )
```

```python
import functools
import math

import jax
import jax.numpy as jnp
from jax import lax
from jax.experimental import pallas as pl
from jax.experimental.pallas import tpu as pltpu
from jax.sharding import PartitionSpec as P


def shifted(block, axis, distance):
    devices = range(lax.axis_size(axis))
    route = [(i - distance, i) for i in devices if i - distance in devices]
    return lax.ppermute(block, axis, route)


def padded(block, sides, width):
    for axis, dim in sides:
        count = lax.axis_size(axis)
        forward = [(i, i + 1) for i in range(count - 1)]
        backward = [(target, source) for source, target in forward]
        low = lax.ppermute(
            lax.slice_in_dim(block, block.shape[dim] - width, None, axis=dim), axis, forward
        )
        high = lax.ppermute(lax.slice_in_dim(block, 0, width, axis=dim), axis, backward)
        block = jnp.concatenate([low, block, high], axis=dim)
    return block


def tap_columns(extended, frame_count, row_count, col_count, flipped):
    pieces = []
    for tap_t in range(3):
        for tap_h in range(3):
            for tap_w in range(3):
                if flipped:
                    start_t, start_h, start_w = (2 - tap_t, 2 - tap_h, 2 - tap_w)
                else:
                    start_t, start_h, start_w = (tap_t, tap_h, tap_w)
                pieces.append(
                    extended[
                        :,
                        start_t : start_t + frame_count,
                        start_h : start_h + row_count,
                        start_w : start_w + col_count,
                        :,
                    ]
                )
    stacked = jnp.concatenate(pieces, axis=-1)
    return stacked.reshape(-1, stacked.shape[-1])


def pad_columns(extended):
    return jnp.pad(extended, ((0, 0), (0, 0), (0, 0), (1, 1), (0, 0)))


MESH = pl.DeviceIdType.MESH


def first_tap(owner, quarter, per, parts):
    return (per * owner - quarter + parts - 1) // parts


def greet(n, parts):
    me_d, me_t, me_s = lax.axis_index("dp"), lax.axis_index("tm"), lax.axis_index("space")
    barrier = pltpu.get_barrier_semaphore()

    def signal(d, t, s):
        pl.semaphore_signal(barrier, inc=1, device_id=(d, t, s), device_id_type=MESH)

    for other in range(1, parts):
        signal(me_d, me_t, lax.rem(me_s + other, parts))
    for other in range(1, n):
        signal(me_d, lax.rem(me_t + other, n), me_s)
    signal(1 - me_d, me_t, me_s)
    pl.semaphore_wait(barrier, parts + n - 1)
    return me_d, me_t, me_s


def shift_columns(block, distance, cols):
    rolled = pltpu.roll(block, distance % block.shape[0], axis=0)
    col = lax.rem(lax.broadcasted_iota(jnp.int32, block.shape, 0), cols)
    edge = 0 if distance > 0 else cols - 1
    return jnp.where(col == edge, 0.0, rolled)


def block_kernel(
    n, parts, per, slots, grad_scale,
    act_ref, pair_ref, rows_ref, next_ref, lat_ref, cot_ref, gain_ref, bias_ref, kernel_hbm,
    out_ref, block_out, latent_grad, vec_out,
    part_ref, from_left, from_right, to_right, to_left, done, vec_ref, vec_plane, vec_line, vec_pair,
    wide_ref, ext_ref, weights, conv_acc, back_acc, conv_mine, conv_send, back_mine, back_send, back_got,
    right_send, right_recv, left_send, left_recv, spread_send, spread_recv, own_sem,
    plane_send, plane_recv, line_send, line_recv, pair_send, pair_recv, swap_send, swap_recv, load_sem,
):
    load = pltpu.make_async_copy(kernel_hbm, weights, load_sem)
    load.start()
    me_d, me_t, me_s = greet(n, parts)
    half = out_ref.shape[-1]
    frames, rows = act_ref.shape[1] // 2, act_ref.shape[2] - 2

    def plane_copy(other):
        return pltpu.make_async_remote_copy(
            src_ref=vec_ref, dst_ref=vec_plane.at[me_s],
            send_sem=plane_send.at[other - 1], recv_sem=plane_recv.at[other - 1],
            device_id=(me_d, me_t, lax.rem(me_s + other, parts)), device_id_type=MESH)

    def line_copy(other):
        return pltpu.make_async_remote_copy(
            src_ref=vec_line.at[me_t], dst_ref=vec_line.at[me_t],
            send_sem=line_send.at[other - 1], recv_sem=line_recv.at[other - 1],
            device_id=(me_d, lax.rem(me_t + other, n), me_s), device_id_type=MESH)

    pair_copy = pltpu.make_async_remote_copy(
        src_ref=vec_pair.at[0], dst_ref=vec_pair.at[1],
        send_sem=pair_send, recv_sem=pair_recv,
        device_id=(1 - me_d, me_t, me_s), device_id_type=MESH)

    cols = act_ref.shape[3]
    own_rows = conv_send.shape[0]
    for clip in range(2):
        flat = rows_ref[clip, :, 1 : 1 + rows].reshape(-1, half)
        exact = flat.astype(jnp.float32)
        wide_ref[clip, :, 0:half] = shift_columns(exact, -1, cols).astype(jnp.bfloat16)
        wide_ref[clip, :, half : 2 * half] = flat
        wide_ref[clip, :, 2 * half :] = shift_columns(exact, 1, cols).astype(jnp.bfloat16)

    def tap_row(group):
        tap_t, tap_h = divmod(group, 3)
        total = None
        for clip in range(2):
            window = act_ref[clip, tap_t : tap_t + frames, tap_h : tap_h + rows]
            term = lax.dot_general(
                window.reshape(-1, window.shape[-1]), wide_ref[clip],
                (((0,), (0,)), ((), ())), preferred_element_type=jnp.float32)
            total = term if total is None else total + term
        total = total * grad_scale
        for tap_w in range(3):
            part_ref[3 * group + tap_w] = total[:, tap_w * half : (tap_w + 1) * half]

    needed = {}
    for dest in range(n):
        for quarter in range(parts):
            for slot in range(slots):
                group = (first_tap(dest, quarter, per, parts) + slot) // 3
                needed[group] = min(slot, needed.get(group, slots))
    for group in range(9):
        if needed[group] == 0:
            tap_row(group)
    part_ref[27] = jnp.zeros_like(part_ref[27])

    small = ext_ref.shape[2]
    ext_ref[:, 0:frames] = rows_ref[:, :, pl.ds(me_s * (small - 2), small)]
    ext_ref[:, frames:] = next_ref[...]
    conv_acc[...] = jnp.zeros_like(conv_acc)
    back_acc[...] = jnp.zeros_like(back_acc)

    def conv_step(group):
        tap_t, tap_h = lax.div(group, 3), lax.rem(group, 3)
        window = pair_ref[:, pl.ds(tap_t, frames), pl.ds(tap_h, small - 2)]
        window = window.reshape(-1, window.shape[-1])
        back = ext_ref[:, pl.ds(2 - tap_t, frames), pl.ds(2 - tap_h, small - 2)]
        back = back.reshape(-1, half)
        for tap_w in range(3):
            block = weights[3 * group + tap_w]
            conv_acc[tap_w] += jnp.dot(window, block, preferred_element_type=jnp.float32)
            back_acc[tap_w] += lax.dot_general(
                back, block, (((1,), (1,)), ((), ())), preferred_element_type=jnp.float32)

    def clip_sum(acc, clip, sign):
        at = pl.ds(pl.multiple_of(clip * own_rows, own_rows), own_rows)
        return (
            shift_columns(acc[0, at], sign, cols)
            + acc[1, at]
            + shift_columns(acc[2, at], -sign, cols)
        )

    conv_swap = pltpu.make_async_remote_copy(
        src_ref=conv_send, dst_ref=conv_mine.at[me_d],
        send_sem=swap_send.at[0], recv_sem=swap_recv.at[0],
        device_id=(1 - me_d, me_t, me_s), device_id_type=MESH)
    back_swap = pltpu.make_async_remote_copy(
        src_ref=back_send, dst_ref=back_got,
        send_sem=swap_send.at[1], recv_sem=swap_recv.at[1],
        device_id=(1 - me_d, me_t, me_s), device_id_type=MESH)

    def start_swaps():
        conv_send[...] = clip_sum(conv_acc, 1 - me_d, 1)
        conv_swap.start()
        back_send[...] = clip_sum(back_acc, 1 - me_d, -1)
        back_swap.start()
        conv_mine[me_d] = clip_sum(conv_acc, me_d, 1)
        back_mine[...] = clip_sum(back_acc, me_d, -1)

    def finish():
        floats = lat_ref[...].astype(jnp.float32)
        grads = cot_ref[...].astype(jnp.float32)
        gain = gain_ref[...]
        conv_swap.wait()
        back_swap.wait()
        conv = jnp.concatenate([conv_mine[0], conv_mine[1]], axis=-1)
        block_out[...] = (floats + conv + bias_ref[...]).astype(jnp.bfloat16)
        scale = lax.rsqrt(jnp.mean(floats * floats, axis=-1, keepdims=True) + 1e-06)
        normed = floats * scale
        pre_act = normed * gain
        sig = 1.0 / (1.0 + jnp.exp(-pre_act))
        pre_grad = (back_mine[...] + back_got[...]) * sig * (1.0 + pre_act * (1.0 - sig))
        normed_grad = pre_grad * gain
        inner = jnp.mean(normed_grad * normed, axis=-1, keepdims=True)
        latent_grad[...] = (grads + scale * (normed_grad - normed * inner)).astype(jnp.bfloat16)
        vec_ref[...] = jnp.zeros_like(vec_ref)
        vec_ref[0:1] = jnp.sum(pre_grad * normed, axis=0, keepdims=True) * grad_scale
        vec_ref[1:2] = jnp.sum(grads, axis=0, keepdims=True) * grad_scale
        for other in range(1, parts):
            plane_copy(other).start()
        vec_plane[me_s] = vec_ref[...]

    def mine(dest, slot):
        return part_ref[first_tap(dest, me_s, per, parts) + slot]

    def right_copy(dest, slot, target):
        return pltpu.make_async_remote_copy(
            src_ref=to_right.at[dest, slot], dst_ref=from_left.at[dest, slot],
            send_sem=right_send.at[dest, slot], recv_sem=right_recv.at[dest, slot],
            device_id=(me_d, target, me_s), device_id_type=MESH)

    def left_copy(dest, slot, target):
        return pltpu.make_async_remote_copy(
            src_ref=to_left.at[dest, slot], dst_ref=from_right.at[dest, slot],
            send_sem=left_send.at[dest, slot], recv_sem=left_recv.at[dest, slot],
            device_id=(me_d, target, me_s), device_id_type=MESH)

    offset = parts * first_tap(me_t, me_s, per, parts) + me_s - per * me_t

    def spread_copy(slot, other):
        unit = parts * slot + offset
        return pltpu.make_async_remote_copy(
            src_ref=done.at[slot], dst_ref=out_ref.at[unit],
            send_sem=spread_send.at[other - 1, slot], recv_sem=spread_recv.at[other - 1, slot],
            device_id=(me_d, me_t, lax.rem(me_s + other, parts)), device_id_type=MESH)

    def step(it, carry):
        r_slot = it - me_t
        l_slot = it - (n - 1 - me_t)
        f_slot = it - n
        for dist in range(n - 1, 0, -1):
            dest_r = me_t + dist
            dest_l = me_t - dist

            @pl.when((dest_r < n) & (r_slot >= 0) & (r_slot < slots))
            def _():
                @pl.when(me_t > 0)
                def _():
                    right_copy(dest_r, r_slot, me_t).wait_recv()
                    to_right[dest_r, r_slot] = (
                        from_left[dest_r, r_slot].astype(jnp.float32) + mine(dest_r, r_slot)
                    ).astype(jnp.bfloat16)

                @pl.when(me_t == 0)
                def _():
                    to_right[dest_r, r_slot] = mine(dest_r, r_slot).astype(jnp.bfloat16)

                right_copy(dest_r, r_slot, me_t + 1).start()

            @pl.when((dest_l >= 0) & (l_slot >= 0) & (l_slot < slots))
            def _():
                @pl.when(me_t < n - 1)
                def _():
                    left_copy(dest_l, l_slot, me_t).wait_recv()
                    to_left[dest_l, l_slot] = (
                        from_right[dest_l, l_slot].astype(jnp.float32) + mine(dest_l, l_slot)
                    ).astype(jnp.bfloat16)

                @pl.when(me_t == n - 1)
                def _():
                    to_left[dest_l, l_slot] = mine(dest_l, l_slot).astype(jnp.bfloat16)

                left_copy(dest_l, l_slot, me_t - 1).start()

        @pl.when((f_slot >= 0) & (f_slot < slots))
        def _():
            @pl.when(me_t == 0)
            def _():
                left_copy(me_t, f_slot, me_t).wait_recv()
                done[f_slot] = (
                    mine(me_t, f_slot) + from_right[me_t, f_slot].astype(jnp.float32)
                ).astype(jnp.bfloat16)

            @pl.when(me_t == n - 1)
            def _():
                right_copy(me_t, f_slot, me_t).wait_recv()
                done[f_slot] = (
                    mine(me_t, f_slot) + from_left[me_t, f_slot].astype(jnp.float32)
                ).astype(jnp.bfloat16)

            @pl.when((me_t > 0) & (me_t < n - 1))
            def _():
                left_copy(me_t, f_slot, me_t).wait_recv()
                right_copy(me_t, f_slot, me_t).wait_recv()
                done[f_slot] = (
                    mine(me_t, f_slot)
                    + from_left[me_t, f_slot].astype(jnp.float32)
                    + from_right[me_t, f_slot].astype(jnp.float32)
                ).astype(jnp.bfloat16)

            for other in range(1, parts):
                spread_copy(f_slot, other).start()
            pltpu.make_async_copy(
                done.at[f_slot], out_ref.at[parts * f_slot + offset], own_sem.at[f_slot]
            ).start()

        for group in range(9):
            if needed[group] > 0:
                pl.when(it == needed[group] - 1)(functools.partial(tap_row, group))

        pl.when(it == 0)(load.wait)
        pl.when(it < 9)(lambda: conv_step(it))
        pl.when(it == last - 1)(start_swaps)
        pl.when(it == last)(finish)
        return carry

    last = max(n + slots - 1, 10)
    lax.fori_loop(0, last + 1, step, 0)

    for other in range(1, parts):
        plane_copy(other).wait()
    vec_line[me_t] = functools.reduce(lambda a, b: a + b, [vec_plane[i] for i in range(parts)])
    for other in range(1, n):
        line_copy(other).start()
    for other in range(1, n):
        line_copy(other).wait()
    vec_pair[0] = functools.reduce(lambda a, b: a + b, [vec_line[i] for i in range(n)])
    pair_copy.start()

    def drain(slot, carry):
        for dist in range(1, n):
            @pl.when(me_t + dist < n)
            def _():
                right_copy(me_t + dist, slot, me_t).wait_send()

            @pl.when(me_t - dist >= 0)
            def _():
                left_copy(me_t - dist, slot, me_t).wait_send()

        for other in range(1, parts):
            spread_copy(slot, other).wait()
        pltpu.make_async_copy(
            done.at[slot], out_ref.at[parts * slot + offset], own_sem.at[slot]
        ).wait()
        return carry

    lax.fori_loop(0, slots, drain, 0)
    pair_copy.wait()
    vec_out[...] = vec_pair[0] + vec_pair[1]


def whole_block(
    act_rows, act_pair, grad_rows, grad_next, latents, out_grad, gain, bias, kernel,
    n, parts, per, slots, grad_scale,
):
    unit, cols = act_rows.shape[-1], kernel.shape[-1]
    chans = latents.shape[-1]
    cells = latents.shape[0]
    frames, all_rows, width = grad_rows.shape[1], grad_rows.shape[2] - 2, grad_rows.shape[3]
    block = (n, slots, unit, cols)
    dma = pltpu.SemaphoreType.DMA
    vmem = pl.BlockSpec(memory_space=pltpu.VMEM)
    low, full = jnp.bfloat16, jnp.float32
    return pl.pallas_call(
        functools.partial(block_kernel, n, parts, per, slots, grad_scale),
        out_shape=(
            jax.ShapeDtypeStruct((parts * slots, unit, cols), low),
            jax.ShapeDtypeStruct((cells, chans), low),
            jax.ShapeDtypeStruct((cells, chans), low),
            jax.ShapeDtypeStruct((8, chans), full),
        ),
        in_specs=[vmem] * 8 + [pl.BlockSpec(memory_space=pl.ANY)],
        out_specs=(vmem,) * 4,
        scratch_shapes=[pltpu.VMEM((28, unit, cols), full)]
        + [pltpu.VMEM(block, low)] * 4
        + [
            pltpu.VMEM((slots, unit, cols), low),
            pltpu.VMEM((8, chans), full),
            pltpu.VMEM((parts, 8, chans), full),
            pltpu.VMEM((n, 8, chans), full),
            pltpu.VMEM((2, 8, chans), full),
            pltpu.VMEM((2, frames * all_rows * width, 3 * cols), low),
            pltpu.VMEM((2, 2 * frames) + grad_next.shape[2:], low),
            pltpu.VMEM(kernel.shape, low),
            pltpu.VMEM((3, 2 * cells, cols), full),
            pltpu.VMEM((3, 2 * cells, chans), full),
            pltpu.VMEM((2, cells, cols), full),
            pltpu.VMEM((cells, cols), full),
            pltpu.VMEM((cells, chans), full),
            pltpu.VMEM((cells, chans), full),
            pltpu.VMEM((cells, chans), full),
        ]
        + [dma((n, slots))] * 4
        + [dma((parts - 1, slots))] * 2
        + [dma((slots,))]
        + [dma((parts - 1,))] * 2
        + [dma((n - 1,))] * 2
        + [dma, dma]
        + [dma((2,)), dma((2,)), dma],
        compiler_params=pltpu.CompilerParams(
            collective_id=0, has_side_effects=True, vmem_limit_bytes=60 * 1024 * 1024
        ),
    )(act_rows, act_pair, grad_rows, grad_next, latents, out_grad, gain, bias, kernel)


def exchange_kernel(n, parts, act_ref, grad_ref, af, aq, gr, gn, send, recv, local):
    me_d, me_t, me_s = greet(n, parts)
    frames, rows, _, chans = act_ref.shape
    half, quarter = gr.shape[-1], aq.shape[-1]
    before, now = pl.ds(0, frames), pl.ds(frames, frames)
    inner = pl.ds(1, rows)
    own = pl.ds(1 + me_s * rows, rows)
    last = 1 + parts * rows

    def channels(index, size):
        return pl.ds(pl.multiple_of(index * size, size), size)

    def remote(i, src, dst, d, t, s):
        return pltpu.make_async_remote_copy(
            src_ref=src, dst_ref=dst, send_sem=send.at[i], recv_sem=recv.at[i],
            device_id=(d, t, s), device_id_type=MESH)

    partner = (1 - me_d, me_t, me_s)
    peers = [lax.rem(me_s + other, parts) for other in range(1, parts)]

    first = 0
    to_partner = remote(
        first, grad_ref.at[:, :, :, channels(1 - me_d, half)], gr.at[me_d, :, own], *partner)
    to_partner.start()
    later = remote(1, act_ref, af.at[me_d, before, inner], me_d, me_t + 1, me_s)

    @pl.when(me_t < n - 1)
    def _():
        later.start()

    def quarter_copy(i, peer, source, when):
        return remote(
            i, source.at[:, :, :, channels(peer, quarter)], aq.at[me_d, when, own],
            me_d, me_t, peer)

    def edge_down(i, source, row, dst):
        return remote(i, source.at[:, row], dst, me_d, me_t, me_s + 1)

    def edge_up(i, source, row, dst):
        return remote(i, source.at[:, row], dst, me_d, me_t, me_s - 1)

    base = 2
    quarters_now = [quarter_copy(base + i, peer, act_ref, now) for i, peer in enumerate(peers)]
    base += parts - 1
    down_now = edge_down(base, act_ref, rows - 1, af.at[me_d, now, 0])
    up_now = edge_up(base + 1, act_ref, 0, af.at[me_d, now, rows + 1])
    base += 2
    own_rows = gr.at[:, :, own]
    gather = [remote(base + i, own_rows, own_rows, me_d, me_t, peer) for i, peer in enumerate(peers)]
    base += parts - 1
    sooner = remote(base, own_rows, gn.at[:, :, inner], me_d, me_t - 1, me_s)
    base += 1
    past = af.at[me_d, before, inner]
    quarters_before = [quarter_copy(base + i, peer, past, before) for i, peer in enumerate(peers)]
    base += parts - 1
    down_before = edge_down(base, past, rows - 1, af.at[me_d, before, 0])
    up_before = edge_up(base + 1, past, 0, af.at[me_d, before, rows + 1])
    base += 2
    down_next = edge_down(base, gn.at[0], rows, gn.at[0, :, 0])
    down_next2 = edge_down(base + 1, gn.at[1], rows, gn.at[1, :, 0])
    up_next = edge_up(base + 2, gn.at[0], 1, gn.at[0, :, rows + 1])
    up_next2 = edge_up(base + 3, gn.at[1], 1, gn.at[1, :, rows + 1])
    base += 4
    forward = [
        remote(base + i, ref.at[me_d, when], ref.at[me_d, when], *partner)
        for i, (ref, when) in enumerate(((aq, now), (af, now), (aq, before), (af, before)))
    ]

    keep = [
        pltpu.make_async_copy(
            grad_ref.at[:, :, :, channels(me_d, half)], gr.at[me_d, :, own], local.at[0]),
        pltpu.make_async_copy(
            act_ref.at[:, :, :, channels(me_s, quarter)], aq.at[me_d, now, own], local.at[1]),
        pltpu.make_async_copy(act_ref, af.at[me_d, now, inner], local.at[2]),
    ]
    keep_before = pltpu.make_async_copy(
        past.at[:, :, :, channels(me_s, quarter)], aq.at[me_d, before, own], local.at[3])

    below, above = me_s < parts - 1, me_s > 0
    for copy in keep:
        copy.start()
    for copy in quarters_now:
        copy.start()

    def start_if(condition, *copies):
        @pl.when(condition)
        def _():
            for copy in copies:
                copy.start()

    start_if(below, down_now)
    start_if(above, up_now)

    def clear(ref, *index):
        ref[index] = jnp.zeros(ref.at[index].shape, ref.dtype)

    everything = slice(None)
    for row in (0, last):
        clear(gr, everything, everything, row)
        clear(aq, me_d, everything, row)

    @pl.when(me_s == 0)
    def _():
        clear(af, me_d, everything, 0)
        clear(gn, everything, everything, 0)

    @pl.when(me_s == parts - 1)
    def _():
        clear(af, me_d, everything, rows + 1)
        clear(gn, everything, everything, rows + 1)

    to_partner.wait_recv()
    keep[0].wait()
    start_if(me_t > 0, sooner)
    for copy in gather:
        copy.start()

    @pl.when(me_t > 0)
    def _():
        later.wait_recv()
        keep_before.start()
        for copy in quarters_before:
            copy.start()
        start_if(below, down_before)
        start_if(above, up_before)

    @pl.when(me_t == 0)
    def _():
        clear(aq, me_d, before, pl.ds(1, parts * rows))
        clear(af, me_d, before, inner)

        @pl.when(above)
        def _():
            clear(af, me_d, before, 0)

        @pl.when(below)
        def _():
            clear(af, me_d, before, rows + 1)

    keep[1].wait()
    keep[2].wait()
    for copy in quarters_now:
        copy.wait_recv()

    def received(condition, *copies):
        @pl.when(condition)
        def _():
            for copy in copies:
                copy.wait_recv()

    received(above, down_now)
    received(below, up_now)
    forward[0].start()
    forward[1].start()

    @pl.when(me_t < n - 1)
    def _():
        sooner.wait_recv()
        start_if(below, down_next, down_next2)
        start_if(above, up_next, up_next2)

    @pl.when(me_t == n - 1)
    def _():
        clear(gn, everything, everything, inner)

        @pl.when(above)
        def _():
            clear(gn, everything, everything, 0)

        @pl.when(below)
        def _():
            clear(gn, everything, everything, rows + 1)

    @pl.when(me_t > 0)
    def _():
        keep_before.wait()
        for copy in quarters_before:
            copy.wait_recv()
        received(above, down_before)
        received(below, up_before)

    forward[2].start()
    forward[3].start()

    @pl.when(me_t < n - 1)
    def _():
        received(above, down_next, down_next2)
        received(below, up_next, up_next2)

    for copy in gather:
        copy.wait_recv()
    for copy in forward:
        copy.wait_recv()

    def sent(condition, *copies):
        @pl.when(condition)
        def _():
            for copy in copies:
                copy.wait_send()

    for copy in [to_partner] + quarters_now + gather + forward:
        copy.wait_send()
    sent(below, down_now)
    sent(above, up_now)
    sent(me_t < n - 1, later)
    sent(me_t > 0, sooner, *quarters_before)
    sent((me_t > 0) & below, down_before)
    sent((me_t > 0) & above, up_before)
    sent((me_t < n - 1) & below, down_next, down_next2)
    sent((me_t < n - 1) & above, up_next, up_next2)


def exchange(act, grad, n, parts):
    frames, rows, cols, chans = act.shape
    half, quarter = chans // 2, chans // parts
    messages = 4 * (parts - 1) + 15
    dma = pltpu.SemaphoreType.DMA
    vmem = pl.BlockSpec(memory_space=pltpu.VMEM)
    return pl.pallas_call(
        functools.partial(exchange_kernel, n, parts),
        out_shape=(
            jax.ShapeDtypeStruct((2, 2 * frames, rows + 2, cols, chans), jnp.bfloat16),
            jax.ShapeDtypeStruct((2, 2 * frames, parts * rows + 2, cols, quarter), jnp.bfloat16),
            jax.ShapeDtypeStruct((2, frames, parts * rows + 2, cols, half), jnp.bfloat16),
            jax.ShapeDtypeStruct((2, frames, rows + 2, cols, half), jnp.bfloat16),
        ),
        in_specs=[vmem] * 2,
        out_specs=(vmem,) * 4,
        scratch_shapes=[dma((messages,)), dma((messages,)), dma((4,))],
        compiler_params=pltpu.CompilerParams(
            collective_id=1, has_side_effects=True, vmem_limit_bytes=32 * 1024 * 1024
        ),
    )(act, grad)


def split_over_space(latents, norm_gain, kernel, conv_bias, out_grad):
    chans, half_cols = latents.shape[-1], kernel.shape[1]
    _, frame_count, row_count, col_count = latents.shape[:4]
    n_tm, n_space = lax.axis_size("tm"), lax.axis_size("space")
    cell_total = frame_count * row_count * col_count * 2 * n_tm * n_space
    grad_scale = 1.0 / math.sqrt(cell_total)
    unit, per = chans // n_space, 27 * n_space // n_tm
    slots = -(-per // n_space)

    floats = latents.astype(jnp.float32)
    scale = lax.rsqrt(jnp.mean(floats * floats, axis=-1, keepdims=True) + 1e-06)
    act = jax.nn.silu(floats * scale * norm_gain).astype(jnp.bfloat16)
    act_pair, act_rows, grad_rows, grad_next = exchange(act[0], out_grad[0], n_tm, n_space)
    spread, block_out, latent_grad, vec = whole_block(
        act_rows, act_pair, grad_rows, grad_next,
        latents.reshape(-1, chans), out_grad.reshape(-1, chans),
        norm_gain.reshape(1, chans), conv_bias.reshape(1, chans),
        kernel.reshape(27, chans, half_cols), n_tm, n_space, per, slots, grad_scale)
    kernel_grad = spread.reshape(-1, half_cols)[: per * unit].astype(jnp.float32)
    return (
        block_out.reshape(latents.shape), latent_grad.reshape(latents.shape), kernel_grad,
        vec[0], vec[1])


def on_device(latents, norm_gain, kernel, conv_bias, out_grad):
    chans = latents.shape[-1]
    n_tm, n_space = lax.axis_size("tm"), lax.axis_size("space")
    splits = (
        lax.axis_size("dp") == 2
        and n_tm > 1
        and n_space > 1
        and latents.shape[:2] == (1, 2)
        and chans % (128 * n_space) == 0
        and chans % 256 == 0
        and latents.shape[3] % 16 == 0
        and 27 * n_space % n_tm == 0
    )
    path = split_over_space if splits else general
    return path(latents, norm_gain, kernel, conv_bias, out_grad)


def general(latents, norm_gain, kernel, conv_bias, out_grad):
    chans = latents.shape[-1]
    half_cols = kernel.shape[1]
    clip_local, frame_count, row_count, col_count = (
        latents.shape[0],
        latents.shape[1],
        latents.shape[2],
        latents.shape[3],
    )
    cell_total = (
        clip_local
        * frame_count
        * row_count
        * col_count
        * lax.axis_size("dp")
        * lax.axis_size("tm")
        * lax.axis_size("space")
    )
    grad_scale = 1.0 / jnp.sqrt(jnp.float32(cell_total))
    floats = latents.astype(jnp.float32)
    scale = lax.rsqrt(jnp.mean(floats * floats, axis=-1, keepdims=True) + 1e-06)
    normed = floats * scale
    pre_act = normed * norm_gain
    act = jax.nn.silu(pre_act).astype(jnp.bfloat16)
    grad_pair = lax.all_to_all(out_grad, "dp", split_axis=4, concat_axis=0, tiled=True)
    earlier = shifted(act, "tm", 1)
    joined = jnp.concatenate([earlier, act], axis=1)
    act_ext = padded(joined, (("space", 2),), 1)
    later = shifted(grad_pair, "tm", -1)
    joined_grad = jnp.concatenate([grad_pair, later], axis=1)
    grad_ext = padded(joined_grad, (("space", 2),), 1)
    act_pair = lax.all_gather(act_ext, "dp", axis=0, tiled=True)
    pair_clips = act_pair.shape[0]
    act_taps = tap_columns(pad_columns(act_pair), frame_count, row_count, col_count, False)
    conv_part = jnp.dot(act_taps, kernel, preferred_element_type=jnp.float32)
    conv_part = conv_part.reshape(pair_clips, frame_count, row_count, col_count, half_cols)
    conv = lax.all_to_all(conv_part, "dp", split_axis=0, concat_axis=4, tiled=True)
    block_out = (floats + conv + conv_bias).astype(jnp.bfloat16)
    kernel_local = (
        lax.dot_general(
            act_taps,
            grad_pair.reshape(-1, half_cols),
            (((0,), (0,)), ((), ())),
            preferred_element_type=jnp.float32,
        )
        * grad_scale
    )
    flipped_kernel = jnp.transpose(kernel.reshape(-1, chans, half_cols), (0, 2, 1)).reshape(
        -1, chans
    )
    grad_taps = tap_columns(pad_columns(grad_ext), frame_count, row_count, col_count, True)
    partial_grad = jnp.dot(grad_taps, flipped_kernel, preferred_element_type=jnp.float32)
    partial_grad = partial_grad.reshape(pair_clips, frame_count, row_count, col_count, chans)
    act_grad = lax.psum_scatter(partial_grad, "dp", scatter_dimension=0, tiled=True)
    grads = out_grad.astype(jnp.float32)
    bias_local = jnp.sum(grads.reshape(-1, chans), axis=0) * grad_scale
    sig = jax.nn.sigmoid(pre_act)
    pre_grad = act_grad * sig * (1.0 + pre_act * (1.0 - sig))
    gain_local = jnp.sum((pre_grad * normed).reshape(-1, chans), axis=0) * grad_scale
    normed_grad = pre_grad * norm_gain
    latent_grad = grads + scale * (
        normed_grad - normed * jnp.mean(normed_grad * normed, axis=-1, keepdims=True)
    )
    gain_grad, bias_grad = lax.psum((gain_local, bias_local), ("dp", "tm", "space"))
    col_part = lax.psum_scatter(kernel_local, "space", scatter_dimension=1, tiled=True)
    cell_part = lax.psum_scatter(col_part, "tm", scatter_dimension=0, tiled=True)
    kernel_grad = lax.all_gather(cell_part, "space", axis=1, tiled=True)
    return (block_out, latent_grad.astype(jnp.bfloat16), kernel_grad, gain_grad, bias_grad)


def solution(mesh):
    in_specs = (
        P("dp", "tm", "space", None, None),
        P(),
        P(None, "dp"),
        P(),
        P("dp", "tm", "space", None, None),
    )
    out_specs = (
        P("dp", "tm", "space", None, None),
        P("dp", "tm", "space", None, None),
        P("tm", "dp"),
        P(),
        P(),
    )
    return jax.shard_map(
        on_device, mesh=mesh, in_specs=in_specs, out_specs=out_specs, check_vma=False
    )
```
